128 devices in a mesh: dp: 32 (over y, z, core), tensor: 4 (over x).
Axes of the slice: x: 4, y: 4, z: 4, core: 2. Of those that a mesh axis runs over, the one named last changes fastest.
Arguments:
- tokens: bfloat16 [4096, 4096], P('dp', 'tensor'), may hold values from -6 to 6
- cotangent: bfloat16 [4096, 4096], P('dp', 'tensor'), may hold values from -6 to 6
- expert_ids: int32 [4096, 8], P('dp'), may hold values from 0 to 63, all different within a row; in each aligned block of 128 rows (0 to 127, 128 to 255, ...) at most 20 rows name the same one
- gates: bfloat16 [4096, 8], P('dp'), may hold values from 0.029907227 to 0.59765625
- w_gate: bfloat16 [64, 4096, 1024], P('dp', None, 'tensor'), may hold values from -0.09375 to 0.09375
- w_up: bfloat16 [64, 4096, 1024], P('dp', None, 'tensor'), may hold values from -0.09375 to 0.09375
- w_down: bfloat16 [64, 1024, 4096], P('dp', 'tensor'), may hold values from -0.1875 to 0.1875
Outputs:
- grad_tokens: bfloat16 [4096, 4096], P('dp', 'tensor')
- grad_gates: bfloat16 [4096, 8], P('dp')
- grad_w_gate: bfloat16 [64, 4096, 1024], P('dp', None, 'tensor')
- grad_w_up: bfloat16 [64, 4096, 1024], P('dp', None, 'tensor')
- grad_w_down: bfloat16 [64, 1024, 4096], P('dp', 'tensor')
The draws below stay inside these ranges and needn't reach their ends.
Inputs may be any that keep to these rules, and one draw needn't show every extreme that they name: `expert_ids`: each token names 8 different experts. Among the tokens of one block of 128, no expert is named more than 20 times, and in every draw some expert is named exactly 20 times in some block.
All inputs are finite; a program needn't handle non-finite values.
Results may differ from the reference program's by a relative error of at most 0.015.
Values may be sent and summed in bfloat16 or wider, within the bound.
No kernel may reach another device: no remote copies, remote signals or barrier semaphores. Data moves between devices by JAX's collectives and lax.ppermute only.
A program may use at most 256 MiB of HBM per device.

```python
import math
import jax
import jax.numpy as jnp
import numpy as np
from jax import lax

D = 4096
FF = 1024
K = 8
TOK_DEV = 128
EXPERTS = 64
CAP = 20
FF_DEV = 256
TOKENS = 4096
N_DP = 32
N_TENSOR = 4


def shard_levels(rng, extent, split, least, high):
    gain = 1.0
    for axis_at, shards_of in split:
        heights = jax.random.uniform(jax.random.fold_in(jax.random.fold_in(rng, 6), axis_at), (shards_of,), jnp.float32, least / len(split), high / len(split))
        gain = gain * jnp.repeat(jnp.exp(heights), extent[axis_at] // shards_of).reshape((-1,) + (1,) * (len(extent) - 1 - axis_at))
    return gain


def deal_out(rng, own, number, rows, count, top, limit, slope):
    sequence = jax.random.permutation(rng, count)
    heavy_load, common = load_shares(count, rows * top, limit, slope, True), load_shares(count, rows * top, limit, slope, False)
    places = jnp.arange(count)

    def named(sizes, turn):
        used = int((sizes > 0).sum())
        fixed = max(1, used // 4)
        shifted = fixed + (places - fixed + turn * (used - fixed)) % max(1, count - fixed)
        return jnp.zeros((count,), jnp.int32).at[sequence[jnp.where(places < fixed, places, shifted)]].set(jnp.asarray(sizes, jnp.int32))

    sizes = jnp.where(number % 4 == 0, named(heavy_load, number // 4), named(common, number - number // 4 - 1))
    mixed = jax.random.permutation(jax.random.fold_in(own, 3), count)
    giver, sink = mixed[0:count // 2 * 2:2], mixed[1:count // 2 * 2:2]
    slack = jnp.minimum(sizes[giver] - 1, limit - sizes[sink]) // 2
    slack = jnp.where((giver == sequence[0]) | (sink == sequence[0]) | (sizes[sink] == 0), 0, jnp.maximum(slack, 0))
    shifted = jax.random.randint(jax.random.fold_in(own, 4), (count // 2,), 0, 1 << 20) % (slack + 1)
    sizes = sizes.at[giver].add(-shifted).at[sink].add(shifted)
    items = jnp.searchsorted(jnp.cumsum(sizes), jnp.arange(rows * top), side="right").astype(jnp.int32)
    grid = items.reshape(top, rows).T
    grid = grid[jax.random.permutation(jax.random.fold_in(own, 1), rows)]
    turn = jax.random.randint(jax.random.fold_in(own, 2), (rows, 1), 0, top)
    return jnp.take_along_axis(grid, (jnp.arange(top)[None, :] + turn) % top, axis=1)


def load_shares(number_of, total, reach, lean, full):
    weights = [(1 << 20) // math.isqrt(rank ** lean) + 1 for rank in range(1, number_of + 1)]
    largest = reach if full else min(reach, max(-(-total // number_of), total * weights[0] // sum(weights)))
    least = 1 if total - largest >= number_of - 1 else 0
    given, spare = [largest] + [least] * (number_of - 1), total - largest - least * (number_of - 1)
    while spare > 0:
        candidates = [i for i in range(1, number_of) if given[i] < largest] or [i for i in range(1, number_of) if given[i] < reach]
        whole, left = sum([weights[i] for i in candidates]), spare
        for i in candidates:
            more = min(reach - given[i], max(1, left * weights[i] // whole), spare)
            given[i] = given[i] + more
            spare = spare - more
    return np.array(given)


def gaussian(own_key, dims, deviation, reach, split=(), held_as=jnp.bfloat16):
    level = shard_levels(own_key, dims, split, -0.22, 0.18) if split else 1.0
    array = jax.random.normal(own_key, dims, jnp.float32) * deviation * level
    return jnp.minimum(jnp.maximum(array, -reach), reach).astype(held_as)


def setup_inputs(seed: int = 0) -> dict:
    arg_keys = jax.random.split(jax.random.key(seed), 8)
    tokens = gaussian(arg_keys[0], (TOKENS, D), 1.0, 6.0, ((0, 32), (1, 4)))
    cotangent = gaussian(arg_keys[1], (TOKENS, D), 1.0, 6.0, ((0, 32), (1, 4)))
    expert_ids_keys = jax.random.split(jax.random.fold_in(arg_keys[2], 1), TOKENS // TOK_DEV)
    expert_ids_turns = jax.random.permutation(jax.random.fold_in(arg_keys[2], 3), TOKENS // TOK_DEV)
    expert_ids = jax.vmap(lambda own, number: deal_out(jax.random.fold_in(arg_keys[2], 2), own, number, TOK_DEV, EXPERTS, K, CAP, 1))(expert_ids_keys, expert_ids_turns).reshape((TOKENS, K))
    gates = jnp.clip(jnp.exp(math.log(0.59765625) - 2.99491561 * jax.random.uniform(arg_keys[3], (TOKENS, K), jnp.float32) ** shard_levels(arg_keys[3], (TOKENS, K), ((0, 32),), -0.2, 0.2)), 0.029907227, 0.59765625).astype(jnp.bfloat16)
    w_gate = gaussian(arg_keys[4], (EXPERTS, D, FF), D ** -0.5, 0.09375, ((0, 32), (2, 4)))
    w_up = gaussian(arg_keys[5], (EXPERTS, D, FF), D ** -0.5, 0.09375, ((0, 32), (2, 4)))
    w_down = gaussian(arg_keys[6], (EXPERTS, FF, D), FF ** -0.5, 0.1875, ((0, 32), (1, 4)))
    return dict(tokens=tokens, cotangent=cotangent, expert_ids=expert_ids, gates=gates, w_gate=w_gate, w_up=w_up, w_down=w_down)


def expert_step(operands):
    x_rows, dy_rows, g_rows, gate_mat, up_mat, down_mat = operands
    h_one = jnp.dot(x_rows, gate_mat, preferred_element_type=jnp.float32)
    h_two = jnp.dot(x_rows, up_mat, preferred_element_type=jnp.float32)
    sigmoid_gate = jax.nn.sigmoid(h_one)
    act = (h_one * sigmoid_gate * h_two).astype(jnp.bfloat16)
    out_rows = jnp.dot(act, down_mat, preferred_element_type=jnp.float32)
    grad_route = jnp.sum(out_rows * dy_rows.astype(jnp.float32), axis=1).astype(jnp.bfloat16)
    dout = (g_rows.astype(jnp.float32)[:, None] * dy_rows.astype(jnp.float32)).astype(jnp.bfloat16)
    grad_down = jnp.dot(act.T, dout, preferred_element_type=jnp.float32).astype(jnp.bfloat16)
    d_act = jnp.dot(dout, down_mat.T, preferred_element_type=jnp.float32)
    d_two = (d_act * h_one * sigmoid_gate).astype(jnp.bfloat16)
    d_one = (d_act * h_two * sigmoid_gate * (1.0 + h_one * (1.0 - sigmoid_gate))).astype(jnp.bfloat16)
    grad_gate = jnp.dot(x_rows.T, d_one, preferred_element_type=jnp.float32).astype(jnp.bfloat16)
    grad_up = jnp.dot(x_rows.T, d_two, preferred_element_type=jnp.float32).astype(jnp.bfloat16)
    total = jnp.zeros((x_rows.shape[0], D), jnp.float32)
    for shard in range(N_TENSOR):
        lo_unit = shard * FF_DEV
        part = jnp.dot(d_one[:, lo_unit:lo_unit + FF_DEV], gate_mat[:, lo_unit:lo_unit + FF_DEV].T, preferred_element_type=jnp.float32)
        part = part + jnp.dot(d_two[:, lo_unit:lo_unit + FF_DEV], up_mat[:, lo_unit:lo_unit + FF_DEV].T, preferred_element_type=jnp.float32)
        total = total + part.astype(jnp.bfloat16).astype(jnp.float32)
    return grad_gate, grad_up, grad_down, total.astype(jnp.bfloat16), grad_route


def reference(tokens, cotangent, expert_ids, gates, w_gate, w_up, w_down):
    route_count = TOK_DEV * K
    rows_each = N_DP * CAP
    flat_ids = expert_ids.reshape(N_DP, route_count).astype(jnp.int32)
    onehot = (flat_ids[:, :, None] == jnp.arange(EXPERTS, dtype=jnp.int32)[None, None, :]).astype(jnp.int32)
    before = jnp.cumsum(onehot, axis=1) - onehot
    slot = jnp.sum(before * onehot, axis=2).astype(jnp.int32)
    source = jnp.arange(N_DP, dtype=jnp.int32)[:, None]
    position = (flat_ids * rows_each + source * CAP + slot).reshape(-1)
    x_rep = jnp.repeat(tokens, K, axis=0)
    dy_rep = jnp.repeat(cotangent, K, axis=0)
    x_buf = jnp.zeros((EXPERTS * rows_each, D), jnp.bfloat16).at[position].set(x_rep).reshape(EXPERTS, rows_each, D)
    dy_buf = jnp.zeros((EXPERTS * rows_each, D), jnp.bfloat16).at[position].set(dy_rep).reshape(EXPERTS, rows_each, D)
    g_buf = jnp.zeros((EXPERTS * rows_each,), jnp.bfloat16).at[position].set(gates.reshape(-1)).reshape(EXPERTS, rows_each)
    grad_gate, grad_up, grad_down, dx_rows, grad_route = lax.map(expert_step, (x_buf, dy_buf, g_buf, w_gate, w_up, w_down))
    back = dx_rows.reshape(EXPERTS * rows_each, D)[position]
    grad_tokens = jnp.sum(back.astype(jnp.float32).reshape(TOKENS, K, D), axis=1).astype(jnp.bfloat16)
    grad_gates = grad_route.reshape(-1)[position].reshape(TOKENS, K)
    return grad_tokens, grad_gates, grad_gate, grad_up, grad_down
```

```python
import functools

import jax
import jax.numpy as jnp
from jax import lax
from jax.experimental import pallas as pl
from jax.experimental.pallas import tpu as pltpu
from jax.sharding import PartitionSpec as P

BF = jnp.bfloat16
F32 = jnp.float32
BLK = 256
NT = (((1,), (1,)), ((), ()))
TN = (((0,), (0,)), ((), ()))
VMEM = 56 * 1024 * 1024


def params():
    return pltpu.CompilerParams(dimension_semantics=("arbitrary",), vmem_limit_bytes=VMEM)


def first_expert(rows, cap):
    return lax.broadcasted_iota(jnp.int32, (rows, 1), 0) % (2 * cap) < cap


def fwd_kernel(per, nq, cap, xq, xp, wg, wu, act, c1, c2, a1, a2):
    i = pl.program_id(0)
    rows = a1.shape[0]

    @pl.when(i == 0)
    def _():
        a1[...] = jnp.zeros_like(a1)
        a2[...] = jnp.zeros_like(a2)

    def add(x):
        for e in range(2):
            at = pl.ds(e * BLK, BLK)
            a1[:, at] += jnp.dot(x, wg[e], preferred_element_type=F32)
            a2[:, at] += jnp.dot(x, wu[e], preferred_element_type=F32)

    @pl.when(i % per < nq)
    def _():
        add(xq[0])

    @pl.when(i % per >= nq)
    def _():
        add(xp[...])

    @pl.when(i == pl.num_programs(0) - 1)
    def _():
        mask = first_expert(rows, cap)
        h1 = jnp.where(mask, a1[:, :BLK], a1[:, BLK:])
        h2 = jnp.where(mask, a2[:, :BLK], a2[:, BLK:])
        s = jax.nn.sigmoid(h1)
        hs = h1 * s
        act[...] = (hs * h2).astype(BF)
        c2[...] = hs
        c1[...] = h2 * s * (1.0 + h1 * (1.0 - s))


def bwd_kernel(per, nq, cap, dq, dp, wd, act, c1, c2, d1, d2, q, acc):
    i = pl.program_id(0)
    rows = acc.shape[0]

    @pl.when(i == 0)
    def _():
        acc[...] = jnp.zeros_like(acc)

    def add(x):
        for e in range(2):
            at = pl.ds(e * BLK, BLK)
            acc[:, at] += lax.dot_general(x, wd[e], NT, preferred_element_type=F32)

    @pl.when(i % per < nq)
    def _():
        add(dq[0])

    @pl.when(i % per >= nq)
    def _():
        add(dp[...])

    @pl.when(i == pl.num_programs(0) - 1)
    def _():
        da = jnp.where(first_expert(rows, cap), acc[:, :BLK], acc[:, BLK:])
        d1[...] = (da * c1[...]).astype(BF)
        d2[...] = (da * c2[...]).astype(BF)
        q[...] = jnp.sum(da * act[...].astype(F32), axis=1, keepdims=True)


def dx_kernel(per, nq, cap, d1, d2, wg, wu, oq, op):
    i = pl.program_id(0)
    mask = first_expert(d1.shape[0], cap)
    zero = jnp.zeros((), BF)

    def part():
        total = None
        for d, w in ((d1, wg), (d2, wu)):
            for e in range(2):
                lhs = jnp.where(mask, d[...], zero) if e == 0 else jnp.where(mask, zero, d[...])
                term = lax.dot_general(lhs, w[e], NT, preferred_element_type=F32)
                total = term if total is None else total + term
        return total.astype(BF)

    @pl.when(i % per < nq)
    def _():
        oq[0] = part()

    @pl.when(i % per >= nq)
    def _():
        op[...] = part()


def grad_kernel(per, nq, cap, xq, xp, dq, dp, d1, d2, act, gg, gu, gd, right, left):
    i = pl.program_id(0)

    @pl.when(i == 0)
    def _():
        mask = first_expert(d1.shape[0], cap)
        zero = jnp.zeros((), BF)
        for at, v in ((0, d1), (2, d2)):
            right[:, at * BLK:(at + 1) * BLK] = jnp.where(mask, v[...], zero)
            right[:, (at + 1) * BLK:(at + 2) * BLK] = jnp.where(mask, zero, v[...])
        left[:BLK] = jnp.where(mask, act[...], zero).T
        left[BLK:] = jnp.where(mask, zero, act[...]).T

    def run(x, d):
        out = lax.dot_general(x, right[...], TN, preferred_element_type=F32).astype(BF)
        gg[0] = out[:, :BLK]
        gg[1] = out[:, BLK:2 * BLK]
        gu[0] = out[:, 2 * BLK:3 * BLK]
        gu[1] = out[:, 3 * BLK:]
        down = jnp.dot(left[...], d, preferred_element_type=F32).astype(BF)
        gd[0] = down[:BLK]
        gd[1] = down[BLK:]

    @pl.when(i % per < nq)
    def _():
        run(xq[0], dq[0])

    @pl.when(i % per >= nq)
    def _():
        run(xp[...], dp[...])


def body(tokens, cotangent, expert_ids, gates, w_gate, w_up, w_down):
    tok, share = tokens.shape
    top = expert_ids.shape[1]
    local, width, ff = w_gate.shape
    n_dp = lax.axis_size("dp")
    n_t = lax.axis_size("tensor")
    experts = local * n_dp
    cap = max(2, tok * top * 5 // (4 * experts))
    rows = experts * cap
    per_dev = local * cap
    per = share // BLK
    nq = per - 1
    qw = nq * BLK
    steps = width // BLK

    eye_e = jnp.arange(experts, dtype=jnp.int32)
    hot = expert_ids[:, :, None] == eye_e[None, None, :]
    names = jnp.sum(hot.astype(F32), axis=1)
    gate_of = jnp.sum(jnp.where(hot, gates.astype(F32)[:, :, None], 0.0), axis=1)
    tri = (jnp.arange(tok)[:, None] > jnp.arange(tok)[None, :]).astype(BF)
    slot = jnp.dot(tri, names.astype(BF), preferred_element_type=F32)
    slot = jnp.where(names > 0, slot, -1.0)
    row_id = jnp.arange(rows, dtype=jnp.int32)
    spread = (row_id[:, None] // cap == eye_e[None, :]).astype(BF)
    slot_rows = lax.dot_general(spread, slot.astype(BF), NT, preferred_element_type=F32)
    gate_rows = lax.dot_general(spread, gate_of.astype(BF), NT, preferred_element_type=F32)
    placed = slot_rows == (row_id % cap).astype(F32)[:, None]
    place = placed.astype(BF)
    place_g = jnp.where(placed, gate_rows, 0.0).astype(BF)

    def to_experts(v):
        v = v.reshape(n_dp, per_dev, v.shape[1])
        return lax.all_to_all(v, "dp", 0, 0, tiled=True).reshape(rows, v.shape[2])

    def rows_of(matrix, v):
        return jnp.dot(matrix, v, preferred_element_type=F32).astype(BF)

    tail = jnp.stack([tokens[:, qw:], cotangent[:, qw:]])
    tail = lax.all_gather(tail, "tensor", axis=2, tiled=True)
    xq = to_experts(rows_of(place, tokens[:, :qw]))
    xq = lax.all_gather(xq, "tensor", axis=0)
    dq = to_experts(rows_of(place_g, cotangent[:, :qw]))
    dq = lax.all_gather(dq, "tensor", axis=0)
    xp = to_experts(rows_of(place, tail[0]))
    dp = to_experts(rows_of(place_g, tail[1]))

    q_spec = pl.BlockSpec((1, rows, BLK), lambda i: (i // per, 0, jnp.minimum(i % per, nq - 1)))
    p_spec = pl.BlockSpec((rows, BLK), lambda i: (0, i // per))
    w_spec = pl.BlockSpec((local, BLK, ff), lambda i: (0, i, 0))
    wd_spec = pl.BlockSpec((local, ff, BLK), lambda i: (0, 0, i))
    whole = pl.BlockSpec((rows, ff), lambda i: (0, 0))
    flops = 2 * 2 * rows * width * ff
    row_bytes = rows * width * 2
    w_bytes = local * width * ff * 2

    act, c1, c2 = pl.pallas_call(
        functools.partial(fwd_kernel, per, nq, cap),
        grid=(steps,),
        in_specs=[q_spec, p_spec, w_spec, w_spec],
        out_specs=[whole, whole, whole],
        out_shape=[
            jax.ShapeDtypeStruct((rows, ff), BF),
            jax.ShapeDtypeStruct((rows, ff), F32),
            jax.ShapeDtypeStruct((rows, ff), F32),
        ],
        scratch_shapes=[pltpu.VMEM((rows, 2 * ff), F32), pltpu.VMEM((rows, 2 * ff), F32)],
        compiler_params=params(),
        cost_estimate=pl.CostEstimate(
            flops=2 * flops, bytes_accessed=row_bytes + 2 * w_bytes, transcendentals=0
        ),
        name="hidden",
    )(xq, xp, w_gate, w_up)

    d1, d2, q = pl.pallas_call(
        functools.partial(bwd_kernel, per, nq, cap),
        grid=(steps,),
        in_specs=[q_spec, p_spec, wd_spec, whole, whole, whole],
        out_specs=[whole, whole, pl.BlockSpec((rows, 1), lambda i: (0, 0))],
        out_shape=[
            jax.ShapeDtypeStruct((rows, ff), BF),
            jax.ShapeDtypeStruct((rows, ff), BF),
            jax.ShapeDtypeStruct((rows, 1), F32),
        ],
        scratch_shapes=[pltpu.VMEM((rows, 2 * ff), F32)],
        compiler_params=params(),
        cost_estimate=pl.CostEstimate(
            flops=flops, bytes_accessed=row_bytes + w_bytes, transcendentals=0
        ),
        name="hidden_grad",
    )(dq, dp, w_down, act, c1, c2)

    oq, op = pl.pallas_call(
        functools.partial(dx_kernel, per, nq, cap),
        grid=(steps,),
        in_specs=[whole, whole, w_spec, w_spec],
        out_specs=[q_spec, p_spec],
        out_shape=[
            jax.ShapeDtypeStruct((n_t, rows, qw), BF),
            jax.ShapeDtypeStruct((rows, n_t * (share - qw)), BF),
        ],
        compiler_params=params(),
        cost_estimate=pl.CostEstimate(
            flops=2 * flops, bytes_accessed=row_bytes + 2 * w_bytes, transcendentals=0
        ),
        name="row_grad",
    )(d1, d2, w_gate, w_up)

    grad_gate, grad_up, grad_down = pl.pallas_call(
        functools.partial(grad_kernel, per, nq, cap),
        grid=(steps,),
        in_specs=[q_spec, p_spec, q_spec, p_spec, whole, whole, whole],
        out_specs=[w_spec, w_spec, wd_spec],
        out_shape=[
            jax.ShapeDtypeStruct(w_gate.shape, BF),
            jax.ShapeDtypeStruct(w_up.shape, BF),
            jax.ShapeDtypeStruct(w_down.shape, BF),
        ],
        scratch_shapes=[pltpu.VMEM((rows, 4 * ff), BF), pltpu.VMEM((2 * ff, rows), BF)],
        compiler_params=params(),
        cost_estimate=pl.CostEstimate(
            flops=3 * flops, bytes_accessed=2 * row_bytes + 3 * w_bytes, transcendentals=0
        ),
        name="weight_grads",
    )(xq, xp, dq, dp, d1, d2, act)

    back_q = to_experts(lax.psum_scatter(oq, "tensor", scatter_dimension=0))
    back_p = to_experts(op)
    q_back = lax.all_to_all(q.reshape(n_dp, per_dev), "dp", 0, 0, tiled=True).reshape(rows, 1)

    tok_q = lax.dot_general(place, back_q, TN, preferred_element_type=F32).astype(BF)
    tok_p = lax.dot_general(place, back_p, TN, preferred_element_type=F32)
    tok_p = lax.psum_scatter(tok_p, "tensor", scatter_dimension=1, tiled=True).astype(BF)
    grad_tokens = jnp.concatenate([tok_q, tok_p], axis=1)

    q_of = lax.dot_general(
        place, (spread.astype(F32) * q_back).astype(BF), TN, preferred_element_type=F32
    )
    q_of = jnp.sum(jnp.where(hot, q_of[:, None, :], 0.0), axis=2)
    grad_gates = (lax.psum(q_of, "tensor") / gates.astype(F32)).astype(BF)
    return grad_tokens, grad_gates, grad_gate, grad_up, grad_down


def solution(mesh):
    in_specs = (
        P("dp", "tensor"),
        P("dp", "tensor"),
        P("dp", None),
        P("dp", None),
        P("dp", None, "tensor"),
        P("dp", None, "tensor"),
        P("dp", "tensor", None),
    )
    out_specs = (
        P("dp", "tensor"),
        P("dp", None),
        P("dp", None, "tensor"),
        P("dp", None, "tensor"),
        P("dp", "tensor", None),
    )
    return jax.shard_map(body, mesh=mesh, in_specs=in_specs, out_specs=out_specs, check_vma=False)
```

```python
import functools

import jax
import jax.numpy as jnp
from jax import lax
from jax.experimental import pallas as pl
from jax.experimental.pallas import tpu as pltpu
from jax.sharding import PartitionSpec as P

BF = jnp.bfloat16
F32 = jnp.float32
BLK = 256
NT = (((1,), (1,)), ((), ()))
TN = (((0,), (0,)), ((), ()))
VMEM = 56 * 1024 * 1024
WHOLE = pl.BlockSpec(memory_space=pltpu.VMEM)
SMEM = pl.BlockSpec(memory_space=pltpu.SMEM)


def params():
    return pltpu.CompilerParams(dimension_semantics=("arbitrary",), vmem_limit_bytes=VMEM)


def cost(flops, nbytes):
    return pl.CostEstimate(flops=flops, bytes_accessed=nbytes, transcendentals=0)


def first_expert(start, rows, cap):
    return (start + lax.broadcasted_iota(jnp.int32, (rows, 1), 0)) % (2 * cap) < cap


def pieces(places, share, n_t, at, refs):
    for place, ref in zip(places, refs):
        column = 0
        for s, device, first, width in place:
            if s is not None:
                device = (at[0] + s) % n_t
            begin = pl.multiple_of(device * share + first, BLK)
            yield ref[:, column:column + width], begin, width
            column += width


def fwd_kernel(places, share, cap, at, *refs):
    xs, (wg, wu, act, act_t, c1, c2) = refs[:-6], refs[-6:]
    rows = act.shape[0]
    sums = [None] * 4
    for x, begin, width in pieces(places, share, wg.shape[1] // share, at, xs):
        for k, (w, e) in enumerate(((wg, 0), (wg, 1), (wu, 0), (wu, 1))):
            term = jnp.dot(x, w[e, pl.ds(begin, width), :], preferred_element_type=F32)
            sums[k] = term if sums[k] is None else sums[k] + term
    mask = first_expert(pl.program_id(0) * rows, rows, cap)
    h1 = jnp.where(mask, sums[0], sums[1])
    h2 = jnp.where(mask, sums[2], sums[3])
    s = jax.nn.sigmoid(h1)
    hs = h1 * s
    a = hs * h2
    act[...] = a.astype(BF)
    act_t[:BLK] = jnp.where(mask, a, 0.0).T.astype(BF)
    act_t[BLK:] = jnp.where(mask, 0.0, a).T.astype(BF)
    c2[...] = hs
    c1[...] = h2 * s * (1.0 + h1 * (1.0 - s))


def bwd_kernel(places, share, cap, at, *refs):
    ds, (wd, act, c1, c2, dh, q) = refs[:-6], refs[-6:]
    rows = ds[0].shape[0]
    sums = [None] * 2
    for d, begin, width in pieces(places, share, wd.shape[2] // share, at, ds):
        for e in range(2):
            w = wd[e, :, pl.ds(begin, width)]
            term = lax.dot_general(d, w, NT, preferred_element_type=F32)
            sums[e] = term if sums[e] is None else sums[e] + term
    mask = first_expert(pl.program_id(0) * rows, rows, cap)
    da = jnp.where(mask, sums[0], sums[1])
    d1 = da * c1[...]
    d2 = da * c2[...]
    for k, v in enumerate((d1, d2)):
        dh[:, 2 * k * BLK:(2 * k + 1) * BLK] = jnp.where(mask, v, 0.0).astype(BF)
        dh[:, (2 * k + 1) * BLK:(2 * k + 2) * BLK] = jnp.where(mask, 0.0, v).astype(BF)
    q[...] = jnp.sum(da * act[...].astype(F32), axis=1, keepdims=True)


def dx_kernel(at, dh, wg, wu, out):
    w = jnp.concatenate([wg[0], wg[1], wu[0], wu[1]], axis=1)
    out[...] = lax.dot_general(dh[...], w, NT, preferred_element_type=F32).astype(BF)


def grad_kernel(nx, nq, at, xq, xp, dq, dp, dh, act_t, *refs):
    gg, gu, gd = refs[-3:]
    i = pl.program_id(0)

    def run(x, d):
        out = lax.dot_general(x[...], dh[...], TN, preferred_element_type=F32).astype(BF)
        gg[0] = out[:, :BLK]
        gg[1] = out[:, BLK:2 * BLK]
        gu[0] = out[:, 2 * BLK:3 * BLK]
        gu[1] = out[:, 3 * BLK:]
        down = jnp.dot(act_t[...], d[...], preferred_element_type=F32).astype(BF)
        gd[0] = down[:BLK]
        gd[1] = down[BLK:]

    @pl.when(i < nx)
    def _():
        run(xq, dq)

    @pl.when((i >= nx) & (i < nq))
    def _():
        run(xp, dq)

    @pl.when(i >= nq)
    def _():
        run(xp, dp)


def body(tokens, cotangent, expert_ids, gates, w_gate, w_up, w_down):
    tok, share = tokens.shape
    top = expert_ids.shape[1]
    local, width, ff = w_gate.shape
    n_dp = lax.axis_size("dp")
    n_t = lax.axis_size("tensor")
    experts = local * n_dp
    cap = max(2, tok * top * 5 // (4 * experts))
    rows = experts * cap
    per_dev = local * cap
    per = share // BLK
    pw = BLK
    qw = share - pw
    nq = qw // BLK
    nx = nq - 1
    qx = nx * BLK
    px = share - qx
    at = lax.axis_index("tensor").astype(jnp.int32).reshape(1)

    def shift(v, s):
        return lax.ppermute(v, "tensor", [(k, (k + s) % n_t) for k in range(n_t)])

    eye_e = jnp.arange(experts, dtype=jnp.int32)
    hot = expert_ids[:, :, None] == eye_e[None, None, :]
    names = jnp.sum(hot.astype(F32), axis=1)
    gate_of = jnp.sum(jnp.where(hot, gates.astype(F32)[:, :, None], 0.0), axis=1)
    tri = (jnp.arange(tok)[:, None] > jnp.arange(tok)[None, :]).astype(BF)
    slot = jnp.dot(tri, names.astype(BF), preferred_element_type=F32)
    slot = jnp.where(names > 0, slot, -1.0)
    row_id = jnp.arange(rows, dtype=jnp.int32)
    spread = (row_id[:, None] // cap == eye_e[None, :]).astype(BF)
    slot_rows = lax.dot_general(spread, slot.astype(BF), NT, preferred_element_type=F32)
    gate_rows = lax.dot_general(spread, gate_of.astype(BF), NT, preferred_element_type=F32)
    placed = slot_rows == (row_id % cap).astype(F32)[:, None]
    place = placed.astype(BF)
    place_g = jnp.where(placed, gate_rows, 0.0).astype(BF)

    def over_dp(v):
        v = v.reshape(n_dp, per_dev, v.shape[1])
        return lax.all_to_all(v, "dp", 0, 0, tiled=True).reshape(rows, v.shape[2])

    def rows_of(matrix, v):
        return jnp.dot(matrix, v, preferred_element_type=F32).astype(BF)

    def after(v, *done):
        return lax.optimization_barrier((v, *done))

    tail = jnp.concatenate([tokens[:, qx:], cotangent[:, qw:]], axis=1)
    tails = [tail] + [shift(tail, -s) for s in range(1, n_t)]
    tail_x = jnp.concatenate([v[:, :px] for v in tails], axis=1)
    tail_d = jnp.concatenate([v[:, px:] for v in tails], axis=1)
    x0 = over_dp(rows_of(place, tokens[:, :qx]))
    sent, x0, tail_x, tail_d = after(rows_of(place_g, cotangent[:, :qw]), x0, tail_x, tail_d)
    xq = lax.all_gather(x0, "tensor", axis=0)
    d0 = over_dp(sent)
    sent, d0 = after(rows_of(place, tail_x), d0)
    dq = lax.all_gather(d0, "tensor", axis=0)
    xp = over_dp(sent)
    sent, xp = after(rows_of(place_g, tail_d), xp)
    dp = over_dp(sent)

    flops = 2 * 2 * rows * width * ff
    row_bytes = rows * width * 2
    w_bytes = local * width * ff * 2
    chunk = BLK
    row_spec = lambda w: pl.BlockSpec((chunk, w), lambda i: (i, 0))
    shape = jax.ShapeDtypeStruct

    def gathered(w):
        return [
            pl.BlockSpec((None, chunk, w), functools.partial(lambda s, i: (s, i, 0), s))
            for s in range(n_t)
        ]

    def places(w):
        return [[(None, s, 0, w)] for s in range(n_t)] + [[(s, 0, w, share - w) for s in range(n_t)]]

    act, act_t, c1, c2 = pl.pallas_call(
        functools.partial(fwd_kernel, places(qx), share, cap),
        grid=(rows // chunk,),
        in_specs=[SMEM] + gathered(qx) + [row_spec(n_t * px), WHOLE, WHOLE],
        out_specs=[
            row_spec(ff),
            pl.BlockSpec((local * ff, chunk), lambda i: (0, i)),
            row_spec(ff),
            row_spec(ff),
        ],
        out_shape=[
            shape((rows, ff), BF),
            shape((local * ff, rows), BF),
            shape((rows, ff), F32),
            shape((rows, ff), F32),
        ],
        compiler_params=params(),
        cost_estimate=cost(2 * flops, row_bytes + 2 * w_bytes),
        name="hidden",
    )(at, *[xq] * n_t, xp, w_gate, w_up)

    dh, q = pl.pallas_call(
        functools.partial(bwd_kernel, places(qw), share, cap),
        grid=(rows // chunk,),
        in_specs=[SMEM] + gathered(qw) + [row_spec(n_t * pw), WHOLE] + [row_spec(ff)] * 3,
        out_specs=[row_spec(4 * ff), row_spec(1)],
        out_shape=[shape((rows, 4 * ff), BF), shape((rows, 1), F32)],
        compiler_params=params(),
        cost_estimate=cost(flops, row_bytes + w_bytes),
        name="hidden_grad",
    )(at, *[dq] * n_t, dp, w_down, act, c1, c2)

    def row_grad(name, dh, steps, w_at, out_spec, out_shape):
        w_spec = pl.BlockSpec((local, BLK, ff), w_at)
        part = n_t * per // steps
        return pl.pallas_call(
            dx_kernel,
            grid_spec=pltpu.PrefetchScalarGridSpec(
                num_scalar_prefetch=1,
                grid=(steps,),
                in_specs=[pl.BlockSpec((rows, 4 * ff), lambda i, ref: (0, 0)), w_spec, w_spec],
                out_specs=out_spec,
            ),
            out_shape=shape(out_shape, BF),
            compiler_params=params(),
            cost_estimate=cost(2 * flops // part, (row_bytes + 2 * w_bytes) // part),
            name=name,
        )(at, dh, w_gate, w_up)

    def shares_grad(name, dh, first, number):
        return row_grad(
            name,
            dh,
            n_t * number,
            lambda i, ref: (0, i // number * per + first + i % number, 0),
            pl.BlockSpec((None, rows, BLK), lambda i, ref: (i // number, 0, i % number)),
            (n_t, rows, number * BLK),
        )

    out_a = shares_grad("row_grad_a", dh, 0, nq - 1)
    dh, out_a = after(dh, out_a)
    p_out = row_grad(
        "row_grad_tail",
        dh,
        n_t,
        lambda i, ref: (0, (ref[0] + i) % n_t * per + nq, 0),
        pl.BlockSpec((rows, BLK), lambda i, ref: (0, i)),
        (rows, n_t * pw),
    )
    dh, p_out = after(dh, p_out)
    out_b = shares_grad("row_grad_b", dh, nq - 1, 1)

    back_p = over_dp(p_out)
    q_back = lax.all_to_all(q.reshape(n_dp, per_dev), "dp", 0, 0, tiled=True).reshape(rows, 1)
    sum_a = lax.psum_scatter(out_a, "tensor", scatter_dimension=0)

    grads = None
    for s in range(n_t):
        w_spec = pl.BlockSpec((local, BLK, ff), lambda i, ref: (0, (ref[0] + s) % n_t * per + i, 0))
        wd_spec = pl.BlockSpec((local, ff, BLK), lambda i, ref: (0, 0, (ref[0] + s) % n_t * per + i))
        def q_spec(n):
            return pl.BlockSpec(
                (None, rows, BLK), lambda i, ref: ((ref[0] + s) % n_t, 0, jnp.minimum(i, n - 1))
            )

        def p_spec(n):
            return pl.BlockSpec(
                (rows, BLK), lambda i, ref: (0, s * (per - n) + jnp.maximum(i - n, 0))
            )

        given = [xq, xp, dq, dp, dh, act_t]
        before = [] if grads is None else list(grads)
        if s == n_t - 1:
            out_b, sum_a, back_p, q_back, *before = after(out_b, sum_a, back_p, q_back, *before)
            back_a = over_dp(sum_a)
            back_b = over_dp(lax.psum_scatter(out_b, "tensor", scatter_dimension=0))
        grads = pl.pallas_call(
            functools.partial(grad_kernel, nx, nq),
            grid_spec=pltpu.PrefetchScalarGridSpec(
                num_scalar_prefetch=1,
                grid=(per,),
                in_specs=[q_spec(nx), p_spec(nx), q_spec(nq), p_spec(nq)]
                + [
                    pl.BlockSpec((rows, 4 * ff), lambda i, ref: (0, 0)),
                    pl.BlockSpec((local * ff, rows), lambda i, ref: (0, 0)),
                ]
                + [pl.BlockSpec(memory_space=pl.ANY)] * len(before),
                out_specs=[w_spec, w_spec, wd_spec],
            ),
            out_shape=[shape(w_gate.shape, BF), shape(w_up.shape, BF), shape(w_down.shape, BF)],
            input_output_aliases={1 + len(given) + k: k for k in range(len(before))},
            compiler_params=params(),
            cost_estimate=cost(3 * flops // n_t, (2 * row_bytes + 3 * w_bytes) // n_t),
            name="weight_grads",
        )(at, *given, *before)
    grad_gate, grad_up, grad_down = grads

    q_of = lax.dot_general(
        place, (spread.astype(F32) * q_back).astype(BF), TN, preferred_element_type=F32
    )
    q_of = jnp.sum(jnp.where(hot, q_of[:, None, :], 0.0), axis=2)
    tok_p = lax.dot_general(place, back_p, TN, preferred_element_type=F32)
    tail_sum, q_sum = tok_p[:, :pw], q_of
    for s in range(1, n_t):
        both = jnp.concatenate(
            [tok_p[:, s * pw:(s + 1) * pw], jnp.pad(q_of, ((0, 0), (0, 128 - top)))], axis=1
        )
        both = shift(both, s)
        tail_sum, q_sum = tail_sum + both[:, :pw], q_sum + both[:, pw:pw + top]
    grad_gates = (q_sum / gates.astype(F32)).astype(BF)
    tok_a = lax.dot_general(place, back_a, TN, preferred_element_type=F32).astype(BF)
    tok_b = lax.dot_general(place, back_b, TN, preferred_element_type=F32).astype(BF)
    grad_tokens = jnp.concatenate([tok_a, tok_b, tail_sum.astype(BF)], axis=1)
    return grad_tokens, grad_gates, grad_gate, grad_up, grad_down


def solution(mesh):
    in_specs = (
        P("dp", "tensor"),
        P("dp", "tensor"),
        P("dp", None),
        P("dp", None),
        P("dp", None, "tensor"),
        P("dp", None, "tensor"),
        P("dp", "tensor", None),
    )
    out_specs = (
        P("dp", "tensor"),
        P("dp", None),
        P("dp", None, "tensor"),
        P("dp", None, "tensor"),
        P("dp", "tensor", None),
    )
    return jax.shard_map(body, mesh=mesh, in_specs=in_specs, out_specs=out_specs, check_vma=False)
```

```python
import functools

import jax
import jax.numpy as jnp
from jax import lax
from jax.experimental import pallas as pl
from jax.experimental.pallas import tpu as pltpu
from jax.sharding import PartitionSpec as P

BF = jnp.bfloat16
F32 = jnp.float32
BLK = 256
NT = (((1,), (1,)), ((), ()))
TN = (((0,), (0,)), ((), ()))
VMEM = 56 * 1024 * 1024
WHOLE = pl.BlockSpec(memory_space=pltpu.VMEM)
SMEM = pl.BlockSpec(memory_space=pltpu.SMEM)


def params():
    return pltpu.CompilerParams(dimension_semantics=("arbitrary",), vmem_limit_bytes=VMEM)


def cost(flops, nbytes):
    return pl.CostEstimate(flops=flops, bytes_accessed=nbytes, transcendentals=0)


def first_expert(start, rows, cap):
    return (start + lax.broadcasted_iota(jnp.int32, (rows, 1), 0)) % (2 * cap) < cap


def pieces(places, share, n_t, at, refs):
    for place, ref in zip(places, refs):
        column = 0
        for s, device, first, width in place:
            if s is not None:
                device = (at[0] + s) % n_t
            begin = pl.multiple_of(device * share + first, BLK)
            yield ref[:, column:column + width], begin, width
            column += width


def fwd_kernel(places, share, cap, at, *refs):
    xs, (wg, wu, act, act_t, c1, c2) = refs[:-6], refs[-6:]
    rows = act.shape[0]
    sums = [None] * 4
    for x, begin, width in pieces(places, share, wg.shape[1] // share, at, xs):
        for k, (w, e) in enumerate(((wg, 0), (wg, 1), (wu, 0), (wu, 1))):
            term = jnp.dot(x, w[e, pl.ds(begin, width), :], preferred_element_type=F32)
            sums[k] = term if sums[k] is None else sums[k] + term
    mask = first_expert(pl.program_id(0) * rows, rows, cap)
    h1 = jnp.where(mask, sums[0], sums[1])
    h2 = jnp.where(mask, sums[2], sums[3])
    s = jax.nn.sigmoid(h1)
    hs = h1 * s
    a = hs * h2
    act[...] = a.astype(BF)
    act_t[:BLK] = jnp.where(mask, a, 0.0).T.astype(BF)
    act_t[BLK:] = jnp.where(mask, 0.0, a).T.astype(BF)
    c2[...] = hs
    c1[...] = h2 * s * (1.0 + h1 * (1.0 - s))


def da_terms(places, share, cap, at, ds, wd):
    rows = ds[0].shape[0]
    sums = [None] * 2
    for d, begin, width in pieces(places, share, wd.shape[2] // share, at, ds):
        for e in range(2):
            w = wd[e, :, pl.ds(begin, width)]
            term = lax.dot_general(d, w, NT, preferred_element_type=F32)
            sums[e] = term if sums[e] is None else sums[e] + term
    mask = first_expert(pl.program_id(0) * rows, rows, cap)
    return mask, jnp.where(mask, sums[0], sums[1])


def bwd_early_kernel(places, share, cap, at, *refs):
    ds, (wd, da) = refs[:-2], refs[-2:]
    da[...] = da_terms(places, share, cap, at, ds, wd)[1]


def bwd_kernel(places, share, cap, at, *refs):
    ds, (wd, early, act, c1, c2, dh, q) = refs[:-7], refs[-7:]
    mask, da = da_terms(places, share, cap, at, ds, wd)
    da = da + early[...]
    d1 = da * c1[...]
    d2 = da * c2[...]
    for k, v in enumerate((d1, d2)):
        dh[:, 2 * k * BLK:(2 * k + 1) * BLK] = jnp.where(mask, v, 0.0).astype(BF)
        dh[:, (2 * k + 1) * BLK:(2 * k + 2) * BLK] = jnp.where(mask, 0.0, v).astype(BF)
    q[...] = jnp.sum(da * act[...].astype(F32), axis=1, keepdims=True)


def dx_kernel(at, dh, wg, wu, out):
    w = jnp.concatenate([wg[0], wg[1], wu[0], wu[1]], axis=1)
    out[...] = lax.dot_general(dh[...], w, NT, preferred_element_type=F32).astype(BF)


def grad_kernel(nx, nq, at, xq, xp, dq, dp, dh, act_t, *refs):
    gg, gu, gd = refs[-3:]
    i = pl.program_id(0)

    def run(x, d):
        out = lax.dot_general(x[...], dh[...], TN, preferred_element_type=F32).astype(BF)
        gg[0] = out[:, :BLK]
        gg[1] = out[:, BLK:2 * BLK]
        gu[0] = out[:, 2 * BLK:3 * BLK]
        gu[1] = out[:, 3 * BLK:]
        down = jnp.dot(act_t[...], d[...], preferred_element_type=F32).astype(BF)
        gd[0] = down[:BLK]
        gd[1] = down[BLK:]

    @pl.when(i < nx)
    def _():
        run(xq, dq)

    @pl.when((i >= nx) & (i < nq))
    def _():
        run(xp, dq)

    @pl.when(i >= nq)
    def _():
        run(xp, dp)


def body(tokens, cotangent, expert_ids, gates, w_gate, w_up, w_down):
    tok, share = tokens.shape
    top = expert_ids.shape[1]
    local, width, ff = w_gate.shape
    n_dp = lax.axis_size("dp")
    n_t = lax.axis_size("tensor")
    experts = local * n_dp
    cap = max(2, tok * top * 5 // (4 * experts))
    rows = experts * cap
    per_dev = local * cap
    per = share // BLK
    pw = BLK
    qw = share - pw
    nq = qw // BLK
    nx = nq - 1
    qx = nx * BLK
    px = share - qx
    at = lax.axis_index("tensor").astype(jnp.int32).reshape(1)

    def shift(v, s):
        return lax.ppermute(v, "tensor", [(k, (k + s) % n_t) for k in range(n_t)])

    eye_e = jnp.arange(experts, dtype=jnp.int32)
    hot = expert_ids[:, :, None] == eye_e[None, None, :]
    names = jnp.sum(hot.astype(F32), axis=1)
    gate_of = jnp.sum(jnp.where(hot, gates.astype(F32)[:, :, None], 0.0), axis=1)
    tri = (jnp.arange(tok)[:, None] > jnp.arange(tok)[None, :]).astype(BF)
    slot = jnp.dot(tri, names.astype(BF), preferred_element_type=F32)
    slot = jnp.where(names > 0, slot, -1.0)
    row_id = jnp.arange(rows, dtype=jnp.int32)
    spread = (row_id[:, None] // cap == eye_e[None, :]).astype(BF)
    slot_rows = lax.dot_general(spread, slot.astype(BF), NT, preferred_element_type=F32)
    gate_rows = lax.dot_general(spread, gate_of.astype(BF), NT, preferred_element_type=F32)
    placed = slot_rows == (row_id % cap).astype(F32)[:, None]
    place = placed.astype(BF)
    place_g = jnp.where(placed, gate_rows, 0.0).astype(BF)

    def over_dp(v):
        v = v.reshape(n_dp, per_dev, v.shape[1])
        return lax.all_to_all(v, "dp", 0, 0, tiled=True).reshape(rows, v.shape[2])

    def rows_of(matrix, v):
        return jnp.dot(matrix, v, preferred_element_type=F32).astype(BF)

    def after(v, *done):
        return lax.optimization_barrier((v, *done))

    tail = jnp.concatenate([tokens[:, qx:], cotangent[:, qw:]], axis=1)
    tails = [tail] + [shift(tail, -s) for s in range(1, n_t)]
    tail_x = jnp.concatenate([v[:, :px] for v in tails], axis=1)
    tail_d = jnp.concatenate([v[:, px:] for v in tails], axis=1)
    x0 = over_dp(rows_of(place, tokens[:, :qx]))
    sent, x0, tail_x, tail_d = after(rows_of(place_g, cotangent[:, :qw]), x0, tail_x, tail_d)
    xq = lax.all_gather(x0, "tensor", axis=0)
    d0 = over_dp(sent)
    sent, d0 = after(rows_of(place, tail_x), d0)
    dq = lax.all_gather(d0, "tensor", axis=0)
    xp = over_dp(sent)
    sent, xp = after(rows_of(place_g, tail_d), xp)
    dp = over_dp(sent)

    flops = 2 * 2 * rows * width * ff
    row_bytes = rows * width * 2
    w_bytes = local * width * ff * 2
    chunk = BLK
    row_spec = lambda w: pl.BlockSpec((chunk, w), lambda i: (i, 0))
    shape = jax.ShapeDtypeStruct

    def gathered(w):
        return [
            pl.BlockSpec((None, chunk, w), functools.partial(lambda s, i: (s, i, 0), s))
            for s in range(n_t)
        ]

    def places(w):
        return [[(None, s, 0, w)] for s in range(n_t)] + [[(s, 0, w, share - w) for s in range(n_t)]]

    act, act_t, c1, c2 = pl.pallas_call(
        functools.partial(fwd_kernel, places(qx), share, cap),
        grid=(rows // chunk,),
        in_specs=[SMEM] + gathered(qx) + [row_spec(n_t * px), WHOLE, WHOLE],
        out_specs=[
            row_spec(ff),
            pl.BlockSpec((local * ff, chunk), lambda i: (0, i)),
            row_spec(ff),
            row_spec(ff),
        ],
        out_shape=[
            shape((rows, ff), BF),
            shape((local * ff, rows), BF),
            shape((rows, ff), F32),
            shape((rows, ff), F32),
        ],
        compiler_params=params(),
        cost_estimate=cost(2 * flops, row_bytes + 2 * w_bytes),
        name="hidden",
    )(at, *[xq] * n_t, xp, w_gate, w_up)

    early = pl.pallas_call(
        functools.partial(bwd_early_kernel, places(qw)[:n_t], share, cap),
        grid=(rows // chunk,),
        in_specs=[SMEM] + gathered(qw) + [WHOLE],
        out_specs=row_spec(ff),
        out_shape=shape((rows, ff), F32),
        compiler_params=params(),
        cost_estimate=cost(flops * 3 // 4, row_bytes * 3 // 4 + w_bytes),
        name="hidden_grad_early",
    )(at, *[dq] * n_t, w_down)
    dh, q = pl.pallas_call(
        functools.partial(bwd_kernel, places(qw)[n_t:], share, cap),
        grid=(rows // chunk,),
        in_specs=[SMEM, row_spec(n_t * pw), WHOLE] + [row_spec(ff)] * 4,
        out_specs=[row_spec(4 * ff), row_spec(1)],
        out_shape=[shape((rows, 4 * ff), BF), shape((rows, 1), F32)],
        compiler_params=params(),
        cost_estimate=cost(flops // 4, row_bytes // 4 + w_bytes),
        name="hidden_grad",
    )(at, dp, w_down, early, act, c1, c2)

    def row_grad(name, dh, steps, w_at, out_spec, out_shape):
        w_spec = pl.BlockSpec((local, BLK, ff), w_at)
        part = n_t * per // steps
        return pl.pallas_call(
            dx_kernel,
            grid_spec=pltpu.PrefetchScalarGridSpec(
                num_scalar_prefetch=1,
                grid=(steps,),
                in_specs=[pl.BlockSpec((rows, 4 * ff), lambda i, ref: (0, 0)), w_spec, w_spec],
                out_specs=out_spec,
            ),
            out_shape=shape(out_shape, BF),
            compiler_params=params(),
            cost_estimate=cost(2 * flops // part, (row_bytes + 2 * w_bytes) // part),
            name=name,
        )(at, dh, w_gate, w_up)

    def shares_grad(name, dh, first, number):
        return row_grad(
            name,
            dh,
            n_t * number,
            lambda i, ref: (0, i // number * per + first + i % number, 0),
            pl.BlockSpec((None, rows, BLK), lambda i, ref: (i // number, 0, i % number)),
            (n_t, rows, number * BLK),
        )

    out_a = shares_grad("row_grad_a", dh, 0, nq - 1)
    dh, out_a = after(dh, out_a)
    p_out = row_grad(
        "row_grad_tail",
        dh,
        n_t,
        lambda i, ref: (0, (ref[0] + i) % n_t * per + nq, 0),
        pl.BlockSpec((rows, BLK), lambda i, ref: (0, i)),
        (rows, n_t * pw),
    )
    dh, p_out = after(dh, p_out)
    out_b = shares_grad("row_grad_b", dh, nq - 1, 1)

    back_p = over_dp(p_out)
    q_back = lax.all_to_all(q.reshape(n_dp, per_dev), "dp", 0, 0, tiled=True).reshape(rows, 1)
    sum_a = lax.psum_scatter(out_a, "tensor", scatter_dimension=0)

    grads = None
    for s in range(n_t):
        w_spec = pl.BlockSpec((local, BLK, ff), lambda i, ref: (0, (ref[0] + s) % n_t * per + i, 0))
        wd_spec = pl.BlockSpec((local, ff, BLK), lambda i, ref: (0, 0, (ref[0] + s) % n_t * per + i))
        def q_spec(n):
            return pl.BlockSpec(
                (None, rows, BLK), lambda i, ref: ((ref[0] + s) % n_t, 0, jnp.minimum(i, n - 1))
            )

        def p_spec(n):
            return pl.BlockSpec(
                (rows, BLK), lambda i, ref: (0, s * (per - n) + jnp.maximum(i - n, 0))
            )

        given = [xq, xp, dq, dp, dh, act_t]
        before = [] if grads is None else list(grads)
        if s == n_t - 1:
            out_b, sum_a, back_p, q_back, *before = after(out_b, sum_a, back_p, q_back, *before)
            back_a = over_dp(sum_a)
            back_b = over_dp(lax.psum_scatter(out_b, "tensor", scatter_dimension=0))
        grads = pl.pallas_call(
            functools.partial(grad_kernel, nx, nq),
            grid_spec=pltpu.PrefetchScalarGridSpec(
                num_scalar_prefetch=1,
                grid=(per,),
                in_specs=[q_spec(nx), p_spec(nx), q_spec(nq), p_spec(nq)]
                + [
                    pl.BlockSpec((rows, 4 * ff), lambda i, ref: (0, 0)),
                    pl.BlockSpec((local * ff, rows), lambda i, ref: (0, 0)),
                ]
                + [pl.BlockSpec(memory_space=pl.ANY)] * len(before),
                out_specs=[w_spec, w_spec, wd_spec],
            ),
            out_shape=[shape(w_gate.shape, BF), shape(w_up.shape, BF), shape(w_down.shape, BF)],
            input_output_aliases={1 + len(given) + k: k for k in range(len(before))},
            compiler_params=params(),
            cost_estimate=cost(3 * flops // n_t, (2 * row_bytes + 3 * w_bytes) // n_t),
            name="weight_grads",
        )(at, *given, *before)
    grad_gate, grad_up, grad_down = grads

    q_of = lax.dot_general(
        place, (spread.astype(F32) * q_back).astype(BF), TN, preferred_element_type=F32
    )
    q_of = jnp.sum(jnp.where(hot, q_of[:, None, :], 0.0), axis=2)
    tok_p = lax.dot_general(place, back_p, TN, preferred_element_type=F32)
    tail_sum, q_sum = tok_p[:, :pw], q_of
    for s in range(1, n_t):
        both = jnp.concatenate(
            [tok_p[:, s * pw:(s + 1) * pw], jnp.pad(q_of, ((0, 0), (0, 128 - top)))], axis=1
        )
        both = shift(both, s)
        tail_sum, q_sum = tail_sum + both[:, :pw], q_sum + both[:, pw:pw + top]
    grad_gates = (q_sum / gates.astype(F32)).astype(BF)
    tok_a = lax.dot_general(place, back_a, TN, preferred_element_type=F32).astype(BF)
    tok_b = lax.dot_general(place, back_b, TN, preferred_element_type=F32).astype(BF)
    grad_tokens = jnp.concatenate([tok_a, tok_b, tail_sum.astype(BF)], axis=1)
    return grad_tokens, grad_gates, grad_gate, grad_up, grad_down


def solution(mesh):
    in_specs = (
        P("dp", "tensor"),
        P("dp", "tensor"),
        P("dp", None),
        P("dp", None),
        P("dp", None, "tensor"),
        P("dp", None, "tensor"),
        P("dp", "tensor", None),
    )
    out_specs = (
        P("dp", "tensor"),
        P("dp", None),
        P("dp", None, "tensor"),
        P("dp", None, "tensor"),
        P("dp", "tensor", None),
    )
    return jax.shard_map(body, mesh=mesh, in_specs=in_specs, out_specs=out_specs, check_vma=False)
```
